32 devices in a mesh: seq: 8 (over z, x), head: 4 (over y, core).
Axes of the slice: x: 2, y: 2, z: 4, core: 2. Of those that a mesh axis runs over, the one named last changes fastest.
Arguments:
- query_rows: bfloat16 [4096, 4096], P('seq', 'head'), may hold values from -6 to 6
- key_rows: bfloat16 [4096, 4096], P('seq', 'head'), may hold values from -6 to 6
- value_rows: bfloat16 [4096, 4096], P('seq', 'head'), may hold values from -19 to 19
- norm_gain: float32 [4096], P('head'), may hold values from 0.5 to 1.5
- out_grad: bfloat16 [4096, 4096], P('seq', 'head'), may hold values from -6 to 6
Outputs:
- attn_out: bfloat16 [4096, 4096], P('seq', 'head')
- grad_query: bfloat16 [4096, 4096], P('seq', 'head')
- grad_key: bfloat16 [4096, 4096], P('seq', 'head')
- grad_value: bfloat16 [4096, 4096], P('seq', 'head')
- grad_gain: float32 [4096], P('head')
The draws below stay inside these ranges and needn't reach their ends.
All inputs are finite; a program needn't handle non-finite values.
Results may differ from the reference program's by a relative error of at most 0.0059.
Values sent between devices are 32-bit elements; how exact they have to be, the bound alone decides.
A program may use at most 128 MiB of HBM per device.

```python
import jax
import jax.numpy as jnp
from jax import lax

HEADS = 32
DH = 128
TOK_DEV = 512
SEQ = 4096
N_SEQ = 8


def draw_value_rows(key, part):
    columns = HEADS * DH
    position = jnp.arange(columns, dtype=jnp.float32) / (columns - 1)
    base = jnp.clip(jax.random.normal(key, (SEQ, columns), jnp.float32), -6.0, 6.0)
    spread = 10.0 ** (0.5 * position)
    return (base * spread[None, :]).astype(jnp.bfloat16)


def level_of(stream_key, dims, cuts, low, largest):
    level, own = 1.0, jax.random.fold_in(stream_key, 6)
    for dim, blocks in cuts:
        draws = jnp.exp(jax.random.uniform(jax.random.fold_in(own, dim), (blocks,), jnp.float32, low / len(cuts), largest / len(cuts)))
        level = level * jnp.repeat(draws, dims[dim] // blocks).reshape([-1 if axis == dim else 1 for axis in range(len(dims))])
    return level


def normal_values(own_key, extent, width, most, cuts=(), kind=jnp.bfloat16):
    drawn = width * jax.random.normal(own_key, extent, jnp.float32)
    if cuts:
        drawn = drawn * level_of(own_key, extent, cuts, -0.22, 0.18)
    return jnp.clip(drawn, -most, most).astype(kind)


def setup_inputs(seed: int = 0) -> dict:
    streams_of = jax.random.split(jax.random.key(seed), 6)
    query_rows = normal_values(streams_of[0], (SEQ, HEADS * DH), 1.0, 6.0, ((0, 8), (1, 4)))
    key_rows = normal_values(streams_of[1], (SEQ, HEADS * DH), 1.0, 6.0, ((0, 8), (1, 4)))
    value_rows = draw_value_rows(jax.random.fold_in(streams_of[5], 71), 0)
    norm_gain = jnp.clip(0.5 + 1.0 * jax.random.uniform(streams_of[3], (HEADS * DH,), jnp.float32) ** level_of(streams_of[3], (HEADS * DH,), ((0, 4),), -0.2, 0.2), 0.5, 1.5)
    out_grad = normal_values(streams_of[4], (SEQ, HEADS * DH), 1.0, 6.0, ((0, 8), (1, 4)))
    return {"query_rows": query_rows, "key_rows": key_rows, "value_rows": value_rows, "norm_gain": norm_gain, "out_grad": out_grad}


norm_eps = 1e-06

def reference(query_rows, key_rows, value_rows, norm_gain, out_grad):
    columns = HEADS * DH
    num_blocks = N_SEQ
    total_rows = num_blocks * TOK_DEV
    query_blocks = query_rows.reshape(num_blocks, TOK_DEV, HEADS, DH)
    key_blocks = key_rows.reshape(num_blocks, TOK_DEV, HEADS, DH)
    value_blocks = value_rows.reshape(num_blocks, TOK_DEV, HEADS, DH)
    causal = jnp.tril(jnp.ones((TOK_DEV, TOK_DEV), dtype=bool))[:, None, :]

    def forward_step(state_sum, pieces):
        query_part, key_part, value_part = pieces
        query_wide = query_part.astype(jnp.float32)
        key_wide = key_part.astype(jnp.float32)
        value_wide = value_part.astype(jnp.float32)
        state_bf = state_sum.astype(jnp.bfloat16)
        scores = jnp.einsum('thd,shd->ths', query_wide, key_wide)
        scores_bf = jnp.where(causal, scores, 0.0).astype(jnp.bfloat16)
        attention = jnp.einsum('thi,hij->thj', query_wide, state_bf.astype(jnp.float32))
        attention = attention + jnp.einsum('ths,shj->thj', scores_bf.astype(jnp.float32), value_wide)
        state_sum = state_sum + jnp.einsum('thi,thj->hij', key_wide, value_wide)
        return (state_sum, (attention, state_bf))
    zero_state = jnp.zeros((HEADS, DH, DH), jnp.float32)
    _, (attention, states_bf) = lax.scan(forward_step, zero_state, (query_blocks, key_blocks, value_blocks))
    attention = attention.reshape(total_rows, columns)
    square_sum = lax.optimization_barrier(jnp.sum(attention * attention, axis=-1))
    inverse = lax.rsqrt(square_sum / columns + norm_eps)
    normed = attention * inverse[:, None]
    attn_out = (normed * norm_gain).astype(jnp.bfloat16)
    grad_wide = out_grad.astype(jnp.float32)
    grad_gain = lax.optimization_barrier(jnp.sum(grad_wide * normed, axis=0))
    scaled = grad_wide * norm_gain
    dot_mean = lax.optimization_barrier(jnp.sum(scaled * attention, axis=-1)) * inverse / columns
    grad_attn = (inverse[:, None] * (scaled - normed * dot_mean[:, None])).astype(jnp.bfloat16)
    grad_blocks = grad_attn.reshape(num_blocks, TOK_DEV, HEADS, DH)

    def backward_step(grad_state, pieces):
        query_part, key_part, value_part, grad_part, state_bf = pieces
        query_wide = query_part.astype(jnp.float32)
        key_wide = key_part.astype(jnp.float32)
        value_wide = value_part.astype(jnp.float32)
        grad_here = grad_part.astype(jnp.float32)
        suffix_bf = grad_state.astype(jnp.bfloat16).astype(jnp.float32)
        scores = jnp.einsum('thd,shd->ths', query_wide, key_wide)
        scores_bf = jnp.where(causal, scores, 0.0).astype(jnp.bfloat16).astype(jnp.float32)
        dscores = jnp.einsum('thj,shj->ths', grad_here, value_wide)
        dscores_bf = jnp.where(causal, dscores, 0.0).astype(jnp.bfloat16).astype(jnp.float32)
        state_wide = state_bf.astype(jnp.float32)
        grad_q = jnp.einsum('thj,hij->thi', grad_here, state_wide) + jnp.einsum('ths,shi->thi', dscores_bf, key_wide)
        grad_k = jnp.einsum('shj,hij->shi', value_wide, suffix_bf) + jnp.einsum('ths,thi->shi', dscores_bf, query_wide)
        grad_v = jnp.einsum('shi,hij->shj', key_wide, suffix_bf) + jnp.einsum('ths,thj->shj', scores_bf, grad_here)
        grad_state = grad_state + jnp.einsum('thi,thj->hij', query_wide, grad_here)
        return (grad_state, (grad_q.astype(jnp.bfloat16), grad_k.astype(jnp.bfloat16), grad_v.astype(jnp.bfloat16)))
    _, (grad_query, grad_key, grad_value) = lax.scan(backward_step, zero_state, (query_blocks, key_blocks, value_blocks, grad_blocks, states_bf), reverse=True)
    grad_query = grad_query.reshape(total_rows, columns)
    grad_key = grad_key.reshape(total_rows, columns)
    grad_value = grad_value.reshape(total_rows, columns)
    return (attn_out, grad_query, grad_key, grad_value, grad_gain)
```

```python
import functools

import jax
import jax.numpy as jnp
from jax import lax
from jax.experimental import pallas as pl
from jax.experimental.pallas import tpu as pltpu
from jax.sharding import PartitionSpec as P

DH = 128
norm_eps = 1e-06
MESH = pl.DeviceIdType.MESH
F32 = jnp.float32
BF16 = jnp.bfloat16


def mm(a, b):
    return lax.dot_general(a, b, (((1,), (0,)), ((), ())), preferred_element_type=F32)


def mm_nt(a, b):
    return lax.dot_general(a, b, (((1,), (1,)), ((), ())), preferred_element_type=F32)


def mm_tn(a, b):
    return lax.dot_general(a, b, (((0,), (0,)), ((), ())), preferred_element_type=F32)


def kernel(
    n_seq, n_head, q_hbm, k_hbm, v_hbm, gain_ref, og_hbm,
    out_hbm, gq_hbm, gk_hbm, gv_hbm, gg_ref,
    q, k, v, og, att, grad, stored, outv, gqv, gkv, gvv, gk_part, gv_part,
    own_f, own_b, xr_f, xr_b, zr_f, zr_b, zs_f, zs_b, ys_f, ys_b, yr_f, yr_b,
    state_bf, stats, stats_in, gain_parts, gain_in,
    load_sem, store_sem, send_f, recv_f, send_b, recv_b,
    head_send, head_recv, gain_send, gain_recv,
):
    me = lax.axis_index("seq")
    hd = lax.axis_index("head")
    rows, width = q.shape
    heads = width // DH
    half = heads // 2
    tile = rows // 2
    columns = width * n_head
    n_outer = n_seq // 2
    outer = me // 2
    inner = me % 2
    partner = me + 1 - 2 * inner
    n_levels = gain_in.shape[0]

    loads = [
        pltpu.make_async_copy(src, dst, load_sem.at[j])
        for j, (src, dst) in enumerate(((k_hbm, k), (v_hbm, v), (q_hbm, q), (og_hbm, og)))
    ]
    for copy in loads:
        copy.start()

    def level_peer(level):
        step = 2 ** level
        bit = (me // step) % 2
        return me + step - 2 * step * bit

    barrier = pltpu.get_barrier_semaphore()
    count = 0
    for r in range(1, n_head):
        pl.semaphore_signal(
            barrier, inc=1, device_id={"head": (hd + r) % n_head}, device_id_type=MESH)
        count += 1
    for level in range(n_levels):
        pl.semaphore_signal(
            barrier, inc=1, device_id={"seq": level_peer(level)}, device_id_type=MESH)
        count += 1

    odd = outer % 2
    third = outer - 1 + 2 * odd
    has_third = jnp.logical_and(third >= 0, third < n_outer)

    @pl.when(has_third)
    def _():
        pl.semaphore_signal(
            barrier, inc=1, device_id={"seq": 2 * third + inner}, device_id_type=MESH)

    def cols(h):
        return pl.ds(pl.multiple_of(h * DH, DH), DH)

    own_base = inner * half
    other_base = (1 - inner) * half

    def remote(src, dst, send, recv, peer):
        return pltpu.make_async_remote_copy(
            src_ref=src, dst_ref=dst, send_sem=send, recv_sem=recv,
            device_id=peer, device_id_type=MESH)

    class Scan:
        def __init__(self, reverse, own, xr, zr, zs, ys, yr, send, recv):
            self.own, self.xr, self.zr, self.zs, self.ys, self.yr = own, xr, zr, zs, ys, yr
            self.send, self.recv = send, recv
            self.at = n_outer - 1 - outer if reverse else outer
            self.side = 1 - inner if reverse else inner
            self.next = me - 2 if reverse else me + 2

        def x(self, j):
            return remote(self.own.at[other_base + j], self.xr.at[j],
                          self.send.at[0, j], self.recv.at[0, j], {"seq": partner})

        def z(self, j):
            return remote(self.zs.at[j], self.zr.at[j],
                          self.send.at[1, j], self.recv.at[1, j], {"seq": self.next})

        def y(self, j):
            return remote(self.ys.at[j], self.yr.at[j],
                          self.send.at[2, j], self.recv.at[2, j], {"seq": partner})

        def clear(self):
            @pl.when(self.at == 0)
            def _():
                self.zr[...] = jnp.zeros_like(self.zr)

        def step(self, j):
            self.x(j).wait_recv()

            @pl.when(self.at > 0)
            def _():
                self.z(j).wait_recv()

            before = self.zr[j]
            mine = self.own[own_base + j]
            theirs = self.xr[j]

            @pl.when(self.at < n_outer - 1)
            def _():
                self.zs[j] = before + (mine + theirs)
                self.z(j).start()

            self.ys[j] = jnp.where(self.side == 0, before + mine, before)
            self.y(j).start()
            return jnp.where(self.side == 0, before, before + theirs)

        def drain(self):
            def body(j, c):
                self.x(j).wait_send()
                self.y(j).wait_send()

                @pl.when(self.at < n_outer - 1)
                def _():
                    self.z(j).wait_send()
                return c
            lax.fori_loop(0, half, body, 0)

    fwd = Scan(False, own_f, xr_f, zr_f, zs_f, ys_f, yr_f, send_f, recv_f)
    bwd = Scan(True, own_b, xr_b, zr_b, zs_b, ys_b, yr_b, send_b, recv_b)
    fwd.clear()
    bwd.clear()

    loads[0].wait()
    loads[1].wait()
    own_f[other_base] = mm_tn(k[:, cols(other_base)], v[:, cols(other_base)])

    pl.semaphore_wait(barrier, jnp.where(has_third, count + 1, count))

    fwd.x(0).start()

    def first_states(j, c):
        h = other_base + j
        own_f[h] = mm_tn(k[:, cols(h)], v[:, cols(h)])
        fwd.x(j).start()
        return c
    lax.fori_loop(1, half, first_states, 0)

    def own_states(j, c):
        h = own_base + j
        own_f[h] = mm_tn(k[:, cols(h)], v[:, cols(h)])
        return c
    lax.fori_loop(0, half, own_states, 0)

    loads[2].wait()
    low = lax.broadcasted_iota(jnp.int32, (tile, tile), 0) >= lax.broadcasted_iota(
        jnp.int32, (tile, tile), 1)
    up = lax.broadcasted_iota(jnp.int32, (tile, tile), 0) <= lax.broadcasted_iota(
        jnp.int32, (tile, tile), 1)

    def keep(mask, x):
        return jnp.where(mask, x, 0.0).astype(BF16)

    def split(ref, h):
        return ref[0:tile, cols(h)], ref[tile:rows, cols(h)]

    def local_fwd(h):
        q0, q1 = split(q, h)
        k0, k1 = split(k, h)
        v0, v1 = split(v, h)
        att[0:tile, cols(h)] = mm(keep(low, mm_nt(q0, k0)), v0)
        att[tile:rows, cols(h)] = mm(mm_nt(q1, k0).astype(BF16), v0) + mm(
            keep(low, mm_nt(q1, k1)), v1)
        stored[h, 0] = keep(up, mm_nt(k0, q0))
        stored[h, 1] = mm_nt(k0, q1).astype(BF16)
        stored[h, 2] = keep(up, mm_nt(k1, q1))

    local_fwd(0)

    def chain_fwd(j, c):
        state_bf[own_base + j] = fwd.step(j).astype(BF16)
        local_fwd(1 + j)
        return c
    lax.fori_loop(0, half, chain_fwd, 0)

    def rest_fwd(h, c):
        local_fwd(h)
        return c
    lax.fori_loop(1 + half, heads, rest_fwd, 0)

    loads[3].wait()

    def attend(h, sums):
        square, dot = sums
        a = att[:, cols(h)] + mm(q[:, cols(h)], state_bf[h])
        att[:, cols(h)] = a
        scaled = og[:, cols(h)].astype(F32) * gain_ref[0:1, cols(h)]
        return square + a * a, dot + scaled * a

    def attend_own(j, sums):
        return attend(own_base + j, sums)

    def attend_other(j, sums):
        fwd.y(j).wait_recv()
        state_bf[other_base + j] = fwd.yr[j].astype(BF16)
        return attend(other_base + j, sums)

    zero = jnp.zeros((rows, DH), F32)
    sums = lax.fori_loop(0, half, attend_own, (zero, zero))
    square, dot = lax.fori_loop(0, half, attend_other, sums)
    lane = lax.broadcasted_iota(jnp.int32, (rows, DH), 1)
    both = jnp.where(lane == 0, jnp.sum(square, axis=1, keepdims=True),
                     jnp.sum(dot, axis=1, keepdims=True))
    stats[...] = jnp.transpose(both)[0:8, :]

    def head_copy(r):
        return remote(stats, stats_in.at[r - 1], head_send.at[r - 1], head_recv.at[r - 1],
                      {"head": (hd + r) % n_head})

    for r in range(1, n_head):
        head_copy(r).start()
    total = stats[...]
    for r in range(1, n_head):
        head_copy(r).wait_recv()
        total = total + stats_in[r - 1]
    total = jnp.transpose(jnp.concatenate([total] * (DH // 8), axis=0))
    inverse = lax.rsqrt(total[:, 0:1] / columns + norm_eps)
    dot_mean = total[:, 1:2] * inverse / columns

    def normalise(h):
        wide = og[:, cols(h)].astype(F32)
        gain = gain_ref[0:1, cols(h)]
        normed = att[:, cols(h)] * inverse
        outv[:, cols(h)] = (normed * gain).astype(BF16)
        part = (wide * normed).reshape(rows // 8, 8, DH)
        gain_parts[0, :, cols(h)] = jnp.sum(part, axis=0)
        g = (inverse * (wide * gain - normed * dot_mean)).astype(BF16)
        grad[:, cols(h)] = g
        own_b[h] = mm_tn(q[:, cols(h)], g)

    def norm_other(j, c):
        normalise(other_base + j)
        bwd.x(j).start()
        return c
    lax.fori_loop(0, half, norm_other, 0)

    def norm_own(j, c):
        normalise(own_base + j)
        return c
    lax.fori_loop(0, half, norm_own, 0)

    out_store = pltpu.make_async_copy(outv, out_hbm, store_sem.at[0])
    out_store.start()

    def gain_copy(level):
        return remote(gain_parts.at[level], gain_in.at[level], gain_send.at[level],
                      gain_recv.at[level], {"seq": level_peer(level)})

    gain_copy(0).start()

    def local_bwd(h):
        q0, q1 = split(q, h)
        k0, k1 = split(k, h)
        v0, v1 = split(v, h)
        g0, g1 = split(grad, h)
        state = state_bf[h]
        gqv[0:tile, cols(h)] = (
            mm_nt(g0, state) + mm(keep(low, mm_nt(g0, v0)), k0)).astype(BF16)
        gqv[tile:rows, cols(h)] = (
            mm_nt(g1, state) + mm(mm_nt(g1, v0).astype(BF16), k0)
            + mm(keep(low, mm_nt(g1, v1)), k1)).astype(BF16)
        gk_part[0:tile, cols(h)] = mm(keep(up, mm_nt(v0, g0)), q0) + mm(
            mm_nt(v0, g1).astype(BF16), q1)
        gk_part[tile:rows, cols(h)] = mm(keep(up, mm_nt(v1, g1)), q1)
        gv_part[0:tile, cols(h)] = mm(stored[h, 0], g0) + mm(stored[h, 1], g1)
        gv_part[tile:rows, cols(h)] = mm(stored[h, 2], g1)

    local_bwd(0)

    def chain_bwd(j, c):
        suffix = bwd.step(j).astype(BF16)
        state_bf[heads + own_base + j] = suffix
        local_bwd(1 + j)
        return c
    lax.fori_loop(0, half, chain_bwd, 0)

    for level in range(n_levels):
        gain_copy(level).wait_recv()
        new = gain_parts[level] + gain_in[level]
        gain_parts[level + 1] = new
        if level < n_levels - 1:
            gain_copy(level + 1).start()
        if 1 + half + level < heads:
            local_bwd(1 + half + level)
    gg_ref[...] = jnp.sum(gain_parts[n_levels], axis=0, keepdims=True)
    for h in range(1 + half + n_levels, heads):
        local_bwd(h)

    gq_store = pltpu.make_async_copy(gqv, gq_hbm, store_sem.at[1])
    gq_store.start()

    def finish(h):
        suffix = state_bf[heads + h]
        gkv[:, cols(h)] = (gk_part[:, cols(h)] + mm_nt(v[:, cols(h)], suffix)).astype(BF16)
        gvv[:, cols(h)] = (gv_part[:, cols(h)] + mm(k[:, cols(h)], suffix)).astype(BF16)

    def finish_own(j, c):
        finish(own_base + j)
        return c
    lax.fori_loop(0, half, finish_own, 0)

    span = half * DH
    own_cols = pl.ds(pl.multiple_of(own_base * DH, span), span)
    other_cols = pl.ds(pl.multiple_of(other_base * DH, span), span)
    stores = [
        pltpu.make_async_copy(src.at[:, c], dst.at[:, c], store_sem.at[2 + n])
        for n, (src, dst, c) in enumerate((
            (gkv, gk_hbm, own_cols), (gvv, gv_hbm, own_cols),
            (gkv, gk_hbm, other_cols), (gvv, gv_hbm, other_cols)))
    ]
    stores[0].start()
    stores[1].start()

    def finish_other(j, c):
        bwd.y(j).wait_recv()
        state_bf[heads + other_base + j] = bwd.yr[j].astype(BF16)
        finish(other_base + j)
        return c
    lax.fori_loop(0, half, finish_other, 0)
    stores[2].start()
    stores[3].start()

    fwd.drain()
    bwd.drain()
    for r in range(1, n_head):
        head_copy(r).wait_send()
    for level in range(n_levels):
        gain_copy(level).wait_send()
    out_store.wait()
    gq_store.wait()
    for copy in stores:
        copy.wait()


def body(n_seq, n_head, query_rows, key_rows, value_rows, norm_gain, out_grad):
    rows, width = query_rows.shape
    heads = width // DH
    half = heads // 2
    tile = rows // 2
    levels = n_seq.bit_length() - 1
    wide = jax.ShapeDtypeStruct((rows, width), BF16)
    vmem = pl.BlockSpec(memory_space=pltpu.VMEM)
    hbm = pl.BlockSpec(memory_space=pl.ANY)
    full = pltpu.VMEM((rows, width), BF16)
    full32 = pltpu.VMEM((rows, width), F32)
    half_states = pltpu.VMEM((half, DH, DH), F32)
    outs = pl.pallas_call(
        functools.partial(kernel, n_seq, n_head),
        out_shape=[wide] * 4 + [jax.ShapeDtypeStruct((1, width), F32)],
        in_specs=[hbm, hbm, hbm, vmem, hbm],
        out_specs=[hbm] * 4 + [vmem],
        scratch_shapes=[full, full, full, full, full32, full,
                        pltpu.VMEM((heads, 3, tile, tile), BF16),
                        full, full, full, full, full32, full32]
        + [pltpu.VMEM((heads, DH, DH), F32)] * 2
        + [half_states] * 10
        + [
            pltpu.VMEM((2 * heads, DH, DH), BF16),
            pltpu.VMEM((8, rows), F32),
            pltpu.VMEM((n_head - 1, 8, rows), F32),
            pltpu.VMEM((levels + 1, 8, width), F32),
            pltpu.VMEM((levels, 8, width), F32),
            pltpu.SemaphoreType.DMA((4,)),
            pltpu.SemaphoreType.DMA((6,)),
            pltpu.SemaphoreType.DMA((3, half)),
            pltpu.SemaphoreType.DMA((3, half)),
            pltpu.SemaphoreType.DMA((3, half)),
            pltpu.SemaphoreType.DMA((3, half)),
            pltpu.SemaphoreType.DMA((n_head - 1,)),
            pltpu.SemaphoreType.DMA((n_head - 1,)),
            pltpu.SemaphoreType.DMA((levels,)),
            pltpu.SemaphoreType.DMA((levels,)),
        ],
        compiler_params=pltpu.CompilerParams(
            collective_id=0, has_side_effects=True, vmem_limit_bytes=48 * 1024 * 1024),
    )(query_rows, key_rows, value_rows, norm_gain.reshape(1, width), out_grad)
    return (*outs[:4], outs[4].reshape(width))


def solution(mesh):
    in_specs = (P("seq", "head"), P("seq", "head"), P("seq", "head"), P("head"), P("seq", "head"))
    out_specs = (P("seq", "head"), P("seq", "head"), P("seq", "head"), P("seq", "head"), P("head"))
    return jax.shard_map(
        functools.partial(body, mesh.shape["seq"], mesh.shape["head"]),
        mesh=mesh, in_specs=in_specs, out_specs=out_specs, check_vma=False)
```

```python
import functools

import jax
import jax.numpy as jnp
from jax import lax
from jax.experimental import pallas as pl
from jax.experimental.pallas import tpu as pltpu
from jax.sharding import PartitionSpec as P

DH = 128
PARTS = 2
PIECE = DH // PARTS
norm_eps = 1e-06
MESH = pl.DeviceIdType.MESH
F32 = jnp.float32
BF16 = jnp.bfloat16


def mm(a, b):
    return lax.dot_general(a, b, (((1,), (0,)), ((), ())), preferred_element_type=F32)


def mm_nt(a, b):
    return lax.dot_general(a, b, (((1,), (1,)), ((), ())), preferred_element_type=F32)


def mm_tn(a, b):
    return lax.dot_general(a, b, (((0,), (0,)), ((), ())), preferred_element_type=F32)


def kernel(
    n_seq, n_head, q_hbm, k_hbm, v_hbm, gain_hbm, og_hbm,
    out_hbm, gq_hbm, gk_hbm, gv_hbm, gg_ref,
    q, k, v, og, gain_ref, att, grad, stored, outv, gqv, gkv, gvv, gk_part, gv_part,
    own_f, own_b, xr_f, xr_b, zr_f, zr_b, zs_f, zs_b, ys_f, ys_b, yr_f, yr_b,
    state_bf, stats, stats_in, gain_parts, gain_in,
    load_sem, store_sem, send_f, recv_f, send_b, recv_b,
    head_send, head_recv, gain_send, gain_recv,
):
    me = lax.axis_index("seq")
    hd = lax.axis_index("head")
    rows, width = q.shape
    heads = width // DH
    half = heads // 2
    tile = rows // 2
    columns = width * n_head
    n_outer = n_seq // 2
    outer = me // 2
    inner = me % 2
    partner = me + 1 - 2 * inner
    n_levels = gain_in.shape[0]

    loads = [
        pltpu.make_async_copy(src, dst, load_sem.at[j])
        for j, (src, dst) in enumerate((
            (k_hbm, k), (v_hbm, v), (q_hbm, q), (og_hbm, og), (gain_hbm, gain_ref)))
    ]
    for copy in loads:
        copy.start()

    def level_peer(level):
        step = 2 ** level
        bit = (me // step) % 2
        return me + step - 2 * step * bit

    barrier = pltpu.get_barrier_semaphore()
    count = 0
    for r in range(1, n_head):
        pl.semaphore_signal(
            barrier, inc=1, device_id={"head": (hd + r) % n_head}, device_id_type=MESH)
        count += 1
    for level in range(n_levels):
        pl.semaphore_signal(
            barrier, inc=1, device_id={"seq": level_peer(level)}, device_id_type=MESH)
        count += 1

    odd = outer % 2
    third = outer - 1 + 2 * odd
    has_third = jnp.logical_and(third >= 0, third < n_outer)

    @pl.when(has_third)
    def _():
        pl.semaphore_signal(
            barrier, inc=1, device_id={"seq": 2 * third + inner}, device_id_type=MESH)

    def cols(h):
        return pl.ds(pl.multiple_of(h * DH, DH), DH)

    own_base = inner * half
    other_base = (1 - inner) * half

    def remote(src, dst, send, recv, peer):
        return pltpu.make_async_remote_copy(
            src_ref=src, dst_ref=dst, send_sem=send, recv_sem=recv,
            device_id=peer, device_id_type=MESH)

    class Scan:
        def __init__(self, reverse, own, xr, zr, zs, ys, yr, send, recv):
            self.own, self.xr, self.zr, self.zs, self.ys, self.yr = own, xr, zr, zs, ys, yr
            self.send, self.recv = send, recv
            self.at = n_outer - 1 - outer if reverse else outer
            self.side = 1 - inner if reverse else inner
            self.next = me - 2 if reverse else me + 2

        def x(self, j, p):
            return remote(self.own.at[other_base + j, p], self.xr.at[j, p],
                          self.send.at[0, j, p], self.recv.at[0, j, p], {"seq": partner})

        def z(self, j, p):
            return remote(self.zs.at[j, p], self.zr.at[j, p],
                          self.send.at[1, j, p], self.recv.at[1, j, p], {"seq": self.next})

        def y(self, j, p):
            return remote(self.ys.at[j, p], self.yr.at[j, p],
                          self.send.at[2, j, p], self.recv.at[2, j, p], {"seq": partner})

        def clear(self):
            @pl.when(self.at == 0)
            def _():
                self.zr[...] = jnp.zeros_like(self.zr)

        def offer(self, j):
            for p in range(PARTS):
                self.x(j, p).start()

        def step(self, j, p):
            self.x(j, p).wait_recv()

            @pl.when(self.at > 0)
            def _():
                self.z(j, p).wait_recv()

            before = self.zr[j, p]
            mine = self.own[own_base + j, p]
            theirs = self.xr[j, p]

            @pl.when(self.at < n_outer - 1)
            def _():
                self.zs[j, p] = before + (mine + theirs)
                self.z(j, p).start()

            self.ys[j, p] = jnp.where(self.side == 0, before + mine, before)
            self.y(j, p).start()
            return jnp.where(self.side == 0, before, before + theirs)

        def chain(self, local, base, between, offset):
            def body(j, c):
                begin = jnp.where(j == 0, 0, jnp.minimum(heads, base + (j - 1) * between))
                lax.fori_loop(begin, jnp.minimum(heads, base + j * between), local, 0)
                for p in range(PARTS):
                    state_bf[offset + own_base + j, p * PIECE:(p + 1) * PIECE] = self.step(
                        j, p).astype(BF16)
                return c
            lax.fori_loop(0, half, body, 0)
            return jnp.minimum(heads, base + (half - 1) * between)

        def arrive(self, j, offset):
            for p in range(PARTS):
                self.y(j, p).wait_recv()
                state_bf[offset + other_base + j, p * PIECE:(p + 1) * PIECE] = self.yr[
                    j, p].astype(BF16)

        def drain(self):
            def body(j, c):
                for p in range(PARTS):
                    self.x(j, p).wait_send()
                    self.y(j, p).wait_send()

                @pl.when(self.at < n_outer - 1)
                def _():
                    for p in range(PARTS):
                        self.z(j, p).wait_send()
                return c
            lax.fori_loop(0, half, body, 0)

    fwd = Scan(False, own_f, xr_f, zr_f, zs_f, ys_f, yr_f, send_f, recv_f)
    bwd = Scan(True, own_b, xr_b, zr_b, zs_b, ys_b, yr_b, send_b, recv_b)
    fwd.clear()
    bwd.clear()

    loads[0].wait()
    loads[1].wait()

    def own_state(h):
        own_f[h] = mm_tn(k[:, cols(h)], v[:, cols(h)]).reshape(PARTS, PIECE, DH)

    own_state(other_base)

    pl.semaphore_wait(barrier, jnp.where(has_third, count + 1, count))

    fwd.offer(0)

    def first_states(j, c):
        h = other_base + j
        own_state(h)
        fwd.offer(j)
        return c
    lax.fori_loop(1, half, first_states, 0)

    def own_states(j, c):
        h = own_base + j
        own_state(h)
        return c
    lax.fori_loop(0, half, own_states, 0)

    loads[2].wait()
    low = lax.broadcasted_iota(jnp.int32, (tile, tile), 0) >= lax.broadcasted_iota(
        jnp.int32, (tile, tile), 1)
    up = lax.broadcasted_iota(jnp.int32, (tile, tile), 0) <= lax.broadcasted_iota(
        jnp.int32, (tile, tile), 1)

    def keep(mask, x):
        return jnp.where(mask, x, 0.0).astype(BF16)

    def split(ref, h):
        return ref[0:tile, cols(h)], ref[tile:rows, cols(h)]

    def local_fwd(h, c):
        q0, q1 = split(q, h)
        k0, k1 = split(k, h)
        v0, v1 = split(v, h)
        att[0:tile, cols(h)] = mm(keep(low, mm_nt(q0, k0)), v0)
        att[tile:rows, cols(h)] = mm(mm_nt(q1, k0).astype(BF16), v0) + mm(
            keep(low, mm_nt(q1, k1)), v1)
        stored[h, 0] = keep(up, mm_nt(k0, q0))
        stored[h, 1] = mm_nt(k0, q1).astype(BF16)
        stored[h, 2] = keep(up, mm_nt(k1, q1))
        return c

    done = fwd.chain(local_fwd, 1 + 2 * fwd.at, 1, 0)
    lax.fori_loop(done, heads, local_fwd, 0)

    loads[3].wait()
    loads[4].wait()

    def attend(h, sums):
        square, dot = sums
        a = att[:, cols(h)] + mm(q[:, cols(h)], state_bf[h])
        att[:, cols(h)] = a
        scaled = og[:, cols(h)].astype(F32) * gain_ref[0:1, cols(h)]
        return square + a * a, dot + scaled * a

    def attend_own(j, sums):
        return attend(own_base + j, sums)

    def attend_other(j, sums):
        fwd.arrive(j, 0)
        return attend(other_base + j, sums)

    zero = jnp.zeros((rows, DH), F32)
    sums = lax.fori_loop(0, half, attend_own, (zero, zero))
    square, dot = lax.fori_loop(0, half, attend_other, sums)
    lane = lax.broadcasted_iota(jnp.int32, (rows, DH), 1)
    both = jnp.where(lane == 0, jnp.sum(square, axis=1, keepdims=True),
                     jnp.sum(dot, axis=1, keepdims=True))
    stats[...] = jnp.transpose(both)[0:8, :]

    def head_copy(r):
        return remote(stats, stats_in.at[r - 1], head_send.at[r - 1], head_recv.at[r - 1],
                      {"head": (hd + r) % n_head})

    for r in range(1, n_head):
        head_copy(r).start()
    total = stats[...]
    for r in range(1, n_head):
        head_copy(r).wait_recv()
        total = total + stats_in[r - 1]
    total = jnp.transpose(jnp.concatenate([total] * (DH // 8), axis=0))
    inverse = lax.rsqrt(total[:, 0:1] / columns + norm_eps)
    dot_mean = total[:, 1:2] * inverse / columns

    def normalise(h):
        wide = og[:, cols(h)].astype(F32)
        gain = gain_ref[0:1, cols(h)]
        normed = att[:, cols(h)] * inverse
        outv[:, cols(h)] = (normed * gain).astype(BF16)
        part = (wide * normed).reshape(rows // 8, 8, DH)
        gain_parts[0, :, cols(h)] = jnp.sum(part, axis=0)
        g = (inverse * (wide * gain - normed * dot_mean)).astype(BF16)
        grad[:, cols(h)] = g
        own_b[h] = mm_tn(q[:, cols(h)], g).reshape(PARTS, PIECE, DH)

    def norm_other(j, c):
        normalise(other_base + j)
        bwd.offer(j)
        return c
    lax.fori_loop(0, half, norm_other, 0)

    def norm_own(j, c):
        normalise(own_base + j)
        return c
    lax.fori_loop(0, half, norm_own, 0)

    out_store = pltpu.make_async_copy(outv, out_hbm, store_sem.at[0])
    out_store.start()

    def gain_copy(level):
        return remote(gain_parts.at[level], gain_in.at[level], gain_send.at[level],
                      gain_recv.at[level], {"seq": level_peer(level)})

    gain_copy(0).start()

    def local_bwd(h, c):
        q0, q1 = split(q, h)
        k0, k1 = split(k, h)
        v0, v1 = split(v, h)
        g0, g1 = split(grad, h)
        state = state_bf[h]
        gqv[0:tile, cols(h)] = (
            mm_nt(g0, state) + mm(keep(low, mm_nt(g0, v0)), k0)).astype(BF16)
        gqv[tile:rows, cols(h)] = (
            mm_nt(g1, state) + mm(mm_nt(g1, v0).astype(BF16), k0)
            + mm(keep(low, mm_nt(g1, v1)), k1)).astype(BF16)
        gk_part[0:tile, cols(h)] = mm(keep(up, mm_nt(v0, g0)), q0) + mm(
            mm_nt(v0, g1).astype(BF16), q1)
        gk_part[tile:rows, cols(h)] = mm(keep(up, mm_nt(v1, g1)), q1)
        gv_part[0:tile, cols(h)] = mm(stored[h, 0], g0) + mm(stored[h, 1], g1)
        gv_part[tile:rows, cols(h)] = mm(stored[h, 2], g1)
        return c

    def gain_level(level):
        gain_copy(level).wait_recv()
        gain_parts[level + 1] = gain_parts[level] + gain_in[level]
        if level < n_levels - 1:
            gain_copy(level + 1).start()

    last = bwd.at == n_outer - 1
    done = bwd.chain(local_bwd, bwd.at, jnp.where(last, 1, 0), heads)
    gain_level(0)
    lax.fori_loop(done, heads, local_bwd, 0)
    for level in range(1, min(2, n_levels)):
        gain_level(level)

    gq_store = pltpu.make_async_copy(gqv, gq_hbm, store_sem.at[1])
    gq_store.start()

    def finish(h):
        suffix = state_bf[heads + h]
        gkv[:, cols(h)] = (gk_part[:, cols(h)] + mm_nt(v[:, cols(h)], suffix)).astype(BF16)
        gvv[:, cols(h)] = (gv_part[:, cols(h)] + mm(k[:, cols(h)], suffix)).astype(BF16)

    def finish_own(j, c):
        finish(own_base + j)
        return c
    lax.fori_loop(0, half, finish_own, 0)

    span = half * DH
    own_cols = pl.ds(pl.multiple_of(own_base * DH, span), span)
    other_cols = pl.ds(pl.multiple_of(other_base * DH, span), span)
    stores = [
        pltpu.make_async_copy(src.at[:, c], dst.at[:, c], store_sem.at[2 + n])
        for n, (src, dst, c) in enumerate((
            (gkv, gk_hbm, own_cols), (gvv, gv_hbm, own_cols),
            (gkv, gk_hbm, other_cols), (gvv, gv_hbm, other_cols)))
    ]
    stores[0].start()
    stores[1].start()

    def finish_other(j, c):
        bwd.arrive(j, heads)
        finish(other_base + j)
        return c
    lax.fori_loop(0, half, finish_other, 0)
    stores[2].start()
    stores[3].start()

    for level in range(2, n_levels):
        gain_level(level)
    gg_ref[...] = jnp.sum(gain_parts[n_levels], axis=0, keepdims=True)

    fwd.drain()
    bwd.drain()
    for r in range(1, n_head):
        head_copy(r).wait_send()
    for level in range(n_levels):
        gain_copy(level).wait_send()
    out_store.wait()
    gq_store.wait()
    for copy in stores:
        copy.wait()


def write_out(*refs):
    sems = refs[10]
    copies = [pltpu.make_async_copy(refs[n], refs[5 + n], sems.at[n]) for n in range(5)]
    for copy in copies:
        copy.start()
    for copy in copies:
        copy.wait()


def body(n_seq, n_head, query_rows, key_rows, value_rows, norm_gain, out_grad):
    rows, width = query_rows.shape
    heads = width // DH
    half = heads // 2
    tile = rows // 2
    levels = n_seq.bit_length() - 1
    wide = jax.ShapeDtypeStruct((rows, width), BF16)
    vmem = pl.BlockSpec(memory_space=pltpu.VMEM)
    hbm = pl.BlockSpec(memory_space=pl.ANY)
    full = pltpu.VMEM((rows, width), BF16)
    full32 = pltpu.VMEM((rows, width), F32)
    half_states = pltpu.VMEM((half, PARTS, PIECE, DH), F32)
    outs = pl.pallas_call(
        functools.partial(kernel, n_seq, n_head),
        out_shape=[wide] * 4 + [jax.ShapeDtypeStruct((1, width), F32)],
        in_specs=[hbm] * 5,
        out_specs=[hbm] * 4 + [vmem],
        scratch_shapes=[full, full, full, full, pltpu.VMEM((1, width), F32), full32, full,
                        pltpu.VMEM((heads, 3, tile, tile), BF16),
                        full, full, full, full, full32, full32]
        + [pltpu.VMEM((heads, PARTS, PIECE, DH), F32)] * 2
        + [half_states] * 10
        + [
            pltpu.VMEM((2 * heads, DH, DH), BF16),
            pltpu.VMEM((8, rows), F32),
            pltpu.VMEM((n_head - 1, 8, rows), F32),
            pltpu.VMEM((levels + 1, 8, width), F32),
            pltpu.VMEM((levels, 8, width), F32),
            pltpu.SemaphoreType.DMA((5,)),
            pltpu.SemaphoreType.DMA((6,)),
            pltpu.SemaphoreType.DMA((3, half, PARTS)),
            pltpu.SemaphoreType.DMA((3, half, PARTS)),
            pltpu.SemaphoreType.DMA((3, half, PARTS)),
            pltpu.SemaphoreType.DMA((3, half, PARTS)),
            pltpu.SemaphoreType.DMA((n_head - 1,)),
            pltpu.SemaphoreType.DMA((n_head - 1,)),
            pltpu.SemaphoreType.DMA((levels,)),
            pltpu.SemaphoreType.DMA((levels,)),
        ],
        compiler_params=pltpu.CompilerParams(
            collective_id=0, has_side_effects=True, vmem_limit_bytes=48 * 1024 * 1024),
    )(query_rows, key_rows, value_rows, norm_gain.reshape(1, width), out_grad)
    outs = pl.pallas_call(
        write_out,
        out_shape=[jax.ShapeDtypeStruct(o.shape, o.dtype) for o in outs],
        in_specs=[hbm] * 5,
        out_specs=[hbm] * 5,
        scratch_shapes=[pltpu.SemaphoreType.DMA((5,))],
        compiler_params=pltpu.CompilerParams(vmem_limit_bytes=1024 * 1024),
    )(*outs)
    return (*outs[:4], outs[4].reshape(width))


def solution(mesh):
    in_specs = (P("seq", "head"), P("seq", "head"), P("seq", "head"), P("head"), P("seq", "head"))
    out_specs = (P("seq", "head"), P("seq", "head"), P("seq", "head"), P("seq", "head"), P("head"))
    return jax.shard_map(
        functools.partial(body, mesh.shape["seq"], mesh.shape["head"]),
        mesh=mesh, in_specs=in_specs, out_specs=out_specs, check_vma=False)
```

```python
import functools

import jax
import jax.numpy as jnp
from jax import lax
from jax.experimental import pallas as pl
from jax.experimental.pallas import tpu as pltpu
from jax.sharding import PartitionSpec as P

DH = 128
PARTS = 2
PIECE = DH // PARTS
norm_eps = 1e-06
MESH = pl.DeviceIdType.MESH
F32 = jnp.float32
BF16 = jnp.bfloat16


def mm(a, b):
    return lax.dot_general(a, b, (((1,), (0,)), ((), ())), preferred_element_type=F32)


def mm_nt(a, b):
    return lax.dot_general(a, b, (((1,), (1,)), ((), ())), preferred_element_type=F32)


def mm_tn(a, b):
    return lax.dot_general(a, b, (((0,), (0,)), ((), ())), preferred_element_type=F32)


def kernel(
    n_seq, n_head, q_hbm, k_hbm, v_hbm, gain_hbm, og_hbm,
    out_hbm, gq_hbm, gk_hbm, gv_hbm, gg_ref,
    q, k, v, og, gain_ref, att, grad, stored, outv, gqv, gkv, gvv, gk_part, gv_part,
    own_f, own_b, xr_f, xr_b, zr_f, zr_b, zs_f, zs_b, ys_f, ys_b, yr_f, yr_b,
    q_turned, inverse_wide, mean_wide, state_bf, stats, stats_in, gain_parts, gain_in,
    load_sem, store_sem, send_f, recv_f, send_b, recv_b,
    head_send, head_recv, gain_send, gain_recv,
):
    me = lax.axis_index("seq")
    hd = lax.axis_index("head")
    rows, width = q.shape
    heads = width // DH
    half = heads // 2
    tile = rows // 2
    columns = width * n_head
    n_outer = n_seq // 2
    outer = me // 2
    inner = me % 2
    partner = me + 1 - 2 * inner
    n_levels = gain_in.shape[0]

    loads = [
        pltpu.make_async_copy(src, dst, load_sem.at[j])
        for j, (src, dst) in enumerate((
            (k_hbm, k), (v_hbm, v), (q_hbm, q), (og_hbm, og), (gain_hbm, gain_ref)))
    ]
    for copy in loads:
        copy.start()

    def level_peer(level):
        step = 2 ** level
        bit = (me // step) % 2
        return me + step - 2 * step * bit

    barrier = pltpu.get_barrier_semaphore()
    count = 0
    for r in range(1, n_head):
        pl.semaphore_signal(
            barrier, inc=1, device_id={"head": (hd + r) % n_head}, device_id_type=MESH)
        count += 1
    for level in range(n_levels):
        pl.semaphore_signal(
            barrier, inc=1, device_id={"seq": level_peer(level)}, device_id_type=MESH)
        count += 1

    odd = outer % 2
    third = outer - 1 + 2 * odd
    has_third = jnp.logical_and(third >= 0, third < n_outer)

    @pl.when(has_third)
    def _():
        pl.semaphore_signal(
            barrier, inc=1, device_id={"seq": 2 * third + inner}, device_id_type=MESH)

    def cols(h):
        return pl.ds(pl.multiple_of(h * DH, DH), DH)

    own_base = inner * half
    other_base = (1 - inner) * half

    def remote(src, dst, send, recv, peer):
        return pltpu.make_async_remote_copy(
            src_ref=src, dst_ref=dst, send_sem=send, recv_sem=recv,
            device_id=peer, device_id_type=MESH)

    class Scan:
        def __init__(self, reverse, own, xr, zr, zs, ys, yr, send, recv):
            self.own, self.xr, self.zr, self.zs, self.ys, self.yr = own, xr, zr, zs, ys, yr
            self.send, self.recv = send, recv
            self.at = n_outer - 1 - outer if reverse else outer
            self.side = 1 - inner if reverse else inner
            self.next = me - 2 if reverse else me + 2

        def x(self, j, p):
            return remote(self.own.at[other_base + j, p], self.xr.at[j, p],
                          self.send.at[0, j, p], self.recv.at[0, j, p], {"seq": partner})

        def z(self, j, p):
            return remote(self.zs.at[j, p], self.zr.at[j, p],
                          self.send.at[1, j, p], self.recv.at[1, j, p], {"seq": self.next})

        def y(self, j, p):
            return remote(self.ys.at[j, p], self.yr.at[j, p],
                          self.send.at[2, j, p], self.recv.at[2, j, p], {"seq": partner})

        def clear(self):
            @pl.when(self.at == 0)
            def _():
                self.zr[...] = jnp.zeros_like(self.zr)

        def offer(self, j):
            for p in range(PARTS):
                self.x(j, p).start()

        def step(self, j, p):
            self.x(j, p).wait_recv()

            @pl.when(self.at > 0)
            def _():
                self.z(j, p).wait_recv()

            before = self.zr[j, p]
            mine = self.own[own_base + j, p]
            theirs = self.xr[j, p]

            @pl.when(self.at < n_outer - 1)
            def _():
                self.zs[j, p] = before + (mine + theirs)
                self.z(j, p).start()

            self.ys[j, p] = jnp.where(self.side == 0, before + mine, before)
            self.y(j, p).start()
            return jnp.where(self.side == 0, before, before + theirs)

        def chain(self, local, units, base, between, offset):
            def body(j, c):
                begin = jnp.where(j == 0, 0, jnp.minimum(units, base + (j - 1) * between))
                lax.fori_loop(begin, jnp.minimum(units, base + j * between), local, 0)
                for p in range(PARTS):
                    state_bf[offset + own_base + j, p * PIECE:(p + 1) * PIECE] = self.step(
                        j, p).astype(BF16)
                return c
            lax.fori_loop(0, half, body, 0)
            return jnp.minimum(units, base + (half - 1) * between)

        def arrive(self, j, offset):
            for p in range(PARTS):
                self.y(j, p).wait_recv()
                state_bf[offset + other_base + j, p * PIECE:(p + 1) * PIECE] = self.yr[
                    j, p].astype(BF16)

        def drain(self):
            def body(j, c):
                for p in range(PARTS):
                    self.x(j, p).wait_send()
                    self.y(j, p).wait_send()

                @pl.when(self.at < n_outer - 1)
                def _():
                    for p in range(PARTS):
                        self.z(j, p).wait_send()
                return c
            lax.fori_loop(0, half, body, 0)

    fwd = Scan(False, own_f, xr_f, zr_f, zs_f, ys_f, yr_f, send_f, recv_f)
    bwd = Scan(True, own_b, xr_b, zr_b, zs_b, ys_b, yr_b, send_b, recv_b)
    fwd.clear()
    bwd.clear()

    loads[0].wait()
    loads[1].wait()

    def own_state(h):
        own_f[h] = mm_tn(k[:, cols(h)], v[:, cols(h)]).reshape(PARTS, PIECE, DH)

    own_state(other_base)

    pl.semaphore_wait(barrier, jnp.where(has_third, count + 1, count))

    fwd.offer(0)

    def first_states(j, c):
        h = other_base + j
        own_state(h)
        fwd.offer(j)
        return c
    lax.fori_loop(1, half, first_states, 0)

    def own_states(j, c):
        h = own_base + j
        own_state(h)
        return c
    lax.fori_loop(0, half, own_states, 0)

    loads[2].wait()
    low = lax.broadcasted_iota(jnp.int32, (tile, tile), 0) >= lax.broadcasted_iota(
        jnp.int32, (tile, tile), 1)
    up = lax.broadcasted_iota(jnp.int32, (tile, tile), 0) <= lax.broadcasted_iota(
        jnp.int32, (tile, tile), 1)

    def keep(mask, x):
        return jnp.where(mask, x, 0.0).astype(BF16)

    def split(ref, h):
        return ref[0:tile, cols(h)], ref[tile:rows, cols(h)]

    def local_fwd(h, c):
        q0, q1 = split(q, h)
        k0, k1 = split(k, h)
        v0, v1 = split(v, h)
        att[0:tile, cols(h)] = mm(keep(low, mm_nt(q0, k0)), v0)
        att[tile:rows, cols(h)] = mm(mm_nt(q1, k0).astype(BF16), v0) + mm(
            keep(low, mm_nt(q1, k1)), v1)
        q_turned[h] = jnp.transpose(q[:, cols(h)])
        stored[h, 0] = keep(up, mm_nt(k0, q0))
        stored[h, 1] = mm_nt(k0, q1).astype(BF16)
        stored[h, 2] = keep(up, mm_nt(k1, q1))
        return c

    done = fwd.chain(local_fwd, heads, 1 + 2 * fwd.at, 1, 0)
    lax.fori_loop(done, heads, local_fwd, 0)

    loads[3].wait()
    loads[4].wait()

    def attend(h, sums):
        square, dot = sums
        a = att[:, cols(h)] + mm(q[:, cols(h)], state_bf[h])
        att[:, cols(h)] = a
        scaled = og[:, cols(h)].astype(F32) * gain_ref[0:1, cols(h)]
        return square + a * a, dot + scaled * a

    def attend_own(j, sums):
        return attend(own_base + j, sums)

    def attend_other(j, sums):
        fwd.arrive(j, 0)
        return attend(other_base + j, sums)

    zero = jnp.zeros((rows, DH), F32)
    sums = lax.fori_loop(0, half, attend_own, (zero, zero))
    square, dot = lax.fori_loop(0, half, attend_other, sums)
    square_row = jnp.sum(jnp.transpose(square), axis=0, keepdims=True)
    dot_row = jnp.sum(jnp.transpose(dot), axis=0, keepdims=True)
    stats[...] = jnp.where(
        lax.broadcasted_iota(jnp.int32, (8, rows), 0) == 0, square_row, dot_row)

    def head_copy(r):
        return remote(stats, stats_in.at[r - 1], head_send.at[r - 1], head_recv.at[r - 1],
                      {"head": (hd + r) % n_head})

    for r in range(1, n_head):
        head_copy(r).start()
    total = stats[...]
    for r in range(1, n_head):
        head_copy(r).wait_recv()
        total = total + stats_in[r - 1]
    inverse = lax.rsqrt(total[0:1, :] / columns + norm_eps)
    dot_mean = total[1:2, :] * inverse / columns
    inverse_wide[...] = jnp.transpose(jnp.broadcast_to(inverse, (DH, rows)))
    mean_wide[...] = jnp.transpose(jnp.broadcast_to(dot_mean, (DH, rows)))

    def normalise(h):
        wide = og[:, cols(h)].astype(F32)
        gain = gain_ref[0:1, cols(h)]
        inv = inverse_wide[...]
        normed = att[:, cols(h)] * inv
        outv[:, cols(h)] = (normed * gain).astype(BF16)
        part = (wide * normed).reshape(rows // 8, 8, DH)
        gain_parts[0, :, cols(h)] = jnp.sum(part, axis=0)
        g = (inv * (wide * gain - normed * mean_wide[...])).astype(BF16)
        grad[:, cols(h)] = g
        own_b[h] = mm(q_turned[h], g).reshape(PARTS, PIECE, DH)

    def norm_other(j, c):
        normalise(other_base + j)
        bwd.offer(j)
        return c
    lax.fori_loop(0, half, norm_other, 0)

    def norm_own(j, c):
        normalise(own_base + j)
        return c
    lax.fori_loop(0, half, norm_own, 0)

    out_store = pltpu.make_async_copy(outv, out_hbm, store_sem.at[0])
    out_store.start()

    def gain_copy(level):
        return remote(gain_parts.at[level], gain_in.at[level], gain_send.at[level],
                      gain_recv.at[level], {"seq": level_peer(level)})

    gain_copy(0).start()

    def value_part(h):
        g0, g1 = split(grad, h)
        gv_part[0:tile, cols(h)] = mm(stored[h, 0], g0) + mm(stored[h, 1], g1)
        gv_part[tile:rows, cols(h)] = mm(stored[h, 2], g1)

    def query_part(h):
        k0, k1 = split(k, h)
        v0, v1 = split(v, h)
        g0, g1 = split(grad, h)
        state = state_bf[h]
        gqv[0:tile, cols(h)] = (
            mm_nt(g0, state) + mm(keep(low, mm_nt(g0, v0)), k0)).astype(BF16)
        gqv[tile:rows, cols(h)] = (
            mm_nt(g1, state) + mm(mm_nt(g1, v0).astype(BF16), k0)
            + mm(keep(low, mm_nt(g1, v1)), k1)).astype(BF16)

    def key_part(h):
        q0, q1 = split(q, h)
        v0, v1 = split(v, h)
        g0, g1 = split(grad, h)
        gk_part[0:tile, cols(h)] = mm(keep(up, mm_nt(v0, g0)), q0) + mm(
            mm_nt(v0, g1).astype(BF16), q1)
        gk_part[tile:rows, cols(h)] = mm(keep(up, mm_nt(v1, g1)), q1)

    units = 3 * heads

    def local_bwd(u, c):
        @pl.when(u < heads)
        def _():
            value_part(u)

        @pl.when(jnp.logical_and(u >= heads, u < 2 * heads))
        def _():
            key_part(u - heads)

        @pl.when(u >= 2 * heads)
        def _():
            query_part(u - 2 * heads)
        return c

    def gain_level(level):
        gain_copy(level).wait_recv()
        gain_parts[level + 1] = gain_parts[level] + gain_in[level]
        if level < n_levels - 1:
            gain_copy(level + 1).start()

    done = bwd.chain(local_bwd, units, 4 * bwd.at, jnp.where(bwd.at == 0, 0, 2), heads)
    gain_level(0)
    lax.fori_loop(done, units, local_bwd, 0)
    for level in range(1, min(2, n_levels)):
        gain_level(level)

    gq_store = pltpu.make_async_copy(gqv, gq_hbm, store_sem.at[1])
    gq_store.start()

    def finish(h):
        suffix = state_bf[heads + h]
        gkv[:, cols(h)] = (gk_part[:, cols(h)] + mm_nt(v[:, cols(h)], suffix)).astype(BF16)
        gvv[:, cols(h)] = (gv_part[:, cols(h)] + mm(k[:, cols(h)], suffix)).astype(BF16)

    def finish_own(j, c):
        finish(own_base + j)
        return c
    lax.fori_loop(0, half, finish_own, 0)

    span = half * DH
    own_cols = pl.ds(pl.multiple_of(own_base * DH, span), span)
    other_cols = pl.ds(pl.multiple_of(other_base * DH, span), span)
    stores = [
        pltpu.make_async_copy(src.at[:, c], dst.at[:, c], store_sem.at[2 + n])
        for n, (src, dst, c) in enumerate((
            (gkv, gk_hbm, own_cols), (gvv, gv_hbm, own_cols),
            (gkv, gk_hbm, other_cols), (gvv, gv_hbm, other_cols)))
    ]
    stores[0].start()
    stores[1].start()

    def finish_other(j, c):
        bwd.arrive(j, heads)
        finish(other_base + j)
        return c
    lax.fori_loop(0, half, finish_other, 0)
    stores[2].start()
    stores[3].start()

    for level in range(2, n_levels):
        gain_level(level)
    gg_ref[...] = jnp.sum(gain_parts[n_levels], axis=0, keepdims=True)

    fwd.drain()
    bwd.drain()
    for r in range(1, n_head):
        head_copy(r).wait_send()
    for level in range(n_levels):
        gain_copy(level).wait_send()
    out_store.wait()
    gq_store.wait()
    for copy in stores:
        copy.wait()


def write_out(*refs):
    sems = refs[10]
    copies = [pltpu.make_async_copy(refs[n], refs[5 + n], sems.at[n]) for n in range(5)]
    for copy in copies:
        copy.start()
    for copy in copies:
        copy.wait()


def body(n_seq, n_head, query_rows, key_rows, value_rows, norm_gain, out_grad):
    rows, width = query_rows.shape
    heads = width // DH
    half = heads // 2
    tile = rows // 2
    levels = n_seq.bit_length() - 1
    wide = jax.ShapeDtypeStruct((rows, width), BF16)
    vmem = pl.BlockSpec(memory_space=pltpu.VMEM)
    hbm = pl.BlockSpec(memory_space=pl.ANY)
    full = pltpu.VMEM((rows, width), BF16)
    full32 = pltpu.VMEM((rows, width), F32)
    half_states = pltpu.VMEM((half, PARTS, PIECE, DH), F32)
    outs = pl.pallas_call(
        functools.partial(kernel, n_seq, n_head),
        out_shape=[wide] * 4 + [jax.ShapeDtypeStruct((1, width), F32)],
        in_specs=[hbm] * 5,
        out_specs=[hbm] * 4 + [vmem],
        scratch_shapes=[full, full, full, full, pltpu.VMEM((1, width), F32), full32, full,
                        pltpu.VMEM((heads, 3, tile, tile), BF16),
                        full, full, full, full, full32, full32]
        + [pltpu.VMEM((heads, PARTS, PIECE, DH), F32)] * 2
        + [half_states] * 10
        + [
            pltpu.VMEM((heads, DH, rows), BF16),
            pltpu.VMEM((rows, DH), F32),
            pltpu.VMEM((rows, DH), F32),
            pltpu.VMEM((2 * heads, DH, DH), BF16),
            pltpu.VMEM((8, rows), F32),
            pltpu.VMEM((n_head - 1, 8, rows), F32),
            pltpu.VMEM((levels + 1, 8, width), F32),
            pltpu.VMEM((levels, 8, width), F32),
            pltpu.SemaphoreType.DMA((5,)),
            pltpu.SemaphoreType.DMA((6,)),
            pltpu.SemaphoreType.DMA((3, half, PARTS)),
            pltpu.SemaphoreType.DMA((3, half, PARTS)),
            pltpu.SemaphoreType.DMA((3, half, PARTS)),
            pltpu.SemaphoreType.DMA((3, half, PARTS)),
            pltpu.SemaphoreType.DMA((n_head - 1,)),
            pltpu.SemaphoreType.DMA((n_head - 1,)),
            pltpu.SemaphoreType.DMA((levels,)),
            pltpu.SemaphoreType.DMA((levels,)),
        ],
        compiler_params=pltpu.CompilerParams(
            collective_id=0, has_side_effects=True, vmem_limit_bytes=48 * 1024 * 1024),
    )(query_rows, key_rows, value_rows, norm_gain.reshape(1, width), out_grad)
    outs = pl.pallas_call(
        write_out,
        out_shape=[jax.ShapeDtypeStruct(o.shape, o.dtype) for o in outs],
        in_specs=[hbm] * 5,
        out_specs=[hbm] * 5,
        scratch_shapes=[pltpu.SemaphoreType.DMA((5,))],
        compiler_params=pltpu.CompilerParams(vmem_limit_bytes=1024 * 1024),
    )(*outs)
    return (*outs[:4], outs[4].reshape(width))


def solution(mesh):
    in_specs = (P("seq", "head"), P("seq", "head"), P("seq", "head"), P("head"), P("seq", "head"))
    out_specs = (P("seq", "head"), P("seq", "head"), P("seq", "head"), P("seq", "head"), P("head"))
    return jax.shard_map(
        functools.partial(body, mesh.shape["seq"], mesh.shape["head"]),
        mesh=mesh, in_specs=in_specs, out_specs=out_specs, check_vma=False)
```

```python
import functools

import jax
import jax.numpy as jnp
from jax import lax
from jax.experimental import pallas as pl
from jax.experimental.pallas import tpu as pltpu
from jax.sharding import PartitionSpec as P

DH = 128
PARTS = 4
PIECE = DH // PARTS
norm_eps = 1e-06
MESH = pl.DeviceIdType.MESH
F32 = jnp.float32
BF16 = jnp.bfloat16


def mm(a, b):
    return lax.dot_general(a, b, (((1,), (0,)), ((), ())), preferred_element_type=F32)


def mm_nt(a, b):
    return lax.dot_general(a, b, (((1,), (1,)), ((), ())), preferred_element_type=F32)


def mm_tn(a, b):
    return lax.dot_general(a, b, (((0,), (0,)), ((), ())), preferred_element_type=F32)


def kernel(
    n_seq, n_head, q_hbm, k_hbm, v_hbm, gain_hbm, og_hbm,
    out_hbm, gq_hbm, gk_hbm, gv_hbm, gg_ref,
    q, k, v, og, gain_ref, att, grad, stored, outv, gqv, gkv, gvv, gk_part, gv_part,
    own_f, own_b, xr_f, xr_b, zr_f, zr_b, zs_f, zs_b, ys_f, ys_b, yr_f, yr_b,
    q_turned, inverse_wide, mean_wide, state_bf, stats, stats_in, gain_parts, gain_in,
    load_sem, store_sem, send_f, recv_f, send_b, recv_b,
    head_send, head_recv, gain_send, gain_recv,
):
    me = lax.axis_index("seq")
    hd = lax.axis_index("head")
    rows, width = q.shape
    heads = width // DH
    half = heads // 2
    tile = rows // 2
    columns = width * n_head
    n_outer = n_seq // 2
    outer = me // 2
    inner = me % 2
    partner = me + 1 - 2 * inner
    n_levels = gain_in.shape[0]

    loads = [
        pltpu.make_async_copy(src, dst, load_sem.at[j])
        for j, (src, dst) in enumerate((
            (k_hbm, k), (v_hbm, v), (q_hbm, q), (og_hbm, og), (gain_hbm, gain_ref)))
    ]
    for copy in loads:
        copy.start()

    def level_peer(level):
        step = 2 ** level
        bit = (me // step) % 2
        return me + step - 2 * step * bit

    barrier = pltpu.get_barrier_semaphore()
    count = 0
    for r in range(1, n_head):
        pl.semaphore_signal(
            barrier, inc=1, device_id={"head": (hd + r) % n_head}, device_id_type=MESH)
        count += 1
    for level in range(n_levels):
        pl.semaphore_signal(
            barrier, inc=1, device_id={"seq": level_peer(level)}, device_id_type=MESH)
        count += 1

    odd = outer % 2
    third = outer - 1 + 2 * odd
    has_third = jnp.logical_and(third >= 0, third < n_outer)

    @pl.when(has_third)
    def _():
        pl.semaphore_signal(
            barrier, inc=1, device_id={"seq": 2 * third + inner}, device_id_type=MESH)

    def cols(h):
        return pl.ds(pl.multiple_of(h * DH, DH), DH)

    own_base = inner * half
    other_base = (1 - inner) * half

    def remote(src, dst, send, recv, peer):
        return pltpu.make_async_remote_copy(
            src_ref=src, dst_ref=dst, send_sem=send, recv_sem=recv,
            device_id=peer, device_id_type=MESH)

    class Scan:
        def __init__(self, reverse, own, xr, zr, zs, ys, yr, send, recv):
            self.own, self.xr, self.zr, self.zs, self.ys, self.yr = own, xr, zr, zs, ys, yr
            self.send, self.recv = send, recv
            self.at = n_outer - 1 - outer if reverse else outer
            self.side = 1 - inner if reverse else inner
            self.next = me - 2 if reverse else me + 2

        def x(self, j, p):
            return remote(self.own.at[other_base + j, p], self.xr.at[j, p],
                          self.send.at[0, j, p], self.recv.at[0, j, p], {"seq": partner})

        def z(self, j, p):
            return remote(self.zs.at[j, p], self.zr.at[j, p],
                          self.send.at[1, j, p], self.recv.at[1, j, p], {"seq": self.next})

        def y(self, j, p):
            return remote(self.ys.at[j, p], self.yr.at[j, p],
                          self.send.at[2, j, p], self.recv.at[2, j, p], {"seq": partner})

        def clear(self):
            @pl.when(self.at == 0)
            def _():
                self.zr[...] = jnp.zeros_like(self.zr)

        def offer(self, j):
            for p in range(PARTS):
                self.x(j, p).start()

        def step(self, j, p):
            self.x(j, p).wait_recv()

            @pl.when(self.at > 0)
            def _():
                self.z(j, p).wait_recv()

            before = self.zr[j, p]
            mine = self.own[own_base + j, p]
            theirs = self.xr[j, p]

            @pl.when(self.at < n_outer - 1)
            def _():
                self.zs[j, p] = before + (mine + theirs)
                self.z(j, p).start()

            self.ys[j, p] = jnp.where(self.side == 0, before + mine, before)
            self.y(j, p).start()
            return jnp.where(self.side == 0, before, before + theirs)

        def chain(self, local, units, base, between, offset):
            def body(j, c):
                begin = jnp.where(j == 0, 0, jnp.minimum(units, base + (j - 1) * between))
                lax.fori_loop(begin, jnp.minimum(units, base + j * between), local, 0)
                for p in range(PARTS):
                    state_bf[offset + own_base + j, p * PIECE:(p + 1) * PIECE] = self.step(
                        j, p).astype(BF16)
                return c
            lax.fori_loop(0, half, body, 0)
            return jnp.minimum(units, base + (half - 1) * between)

        def arrive(self, j, offset):
            for p in range(PARTS):
                self.y(j, p).wait_recv()
                state_bf[offset + other_base + j, p * PIECE:(p + 1) * PIECE] = self.yr[
                    j, p].astype(BF16)

        def drain(self):
            def body(j, c):
                for p in range(PARTS):
                    self.x(j, p).wait_send()
                    self.y(j, p).wait_send()

                @pl.when(self.at < n_outer - 1)
                def _():
                    for p in range(PARTS):
                        self.z(j, p).wait_send()
                return c
            lax.fori_loop(0, half, body, 0)

    fwd = Scan(False, own_f, xr_f, zr_f, zs_f, ys_f, yr_f, send_f, recv_f)
    bwd = Scan(True, own_b, xr_b, zr_b, zs_b, ys_b, yr_b, send_b, recv_b)
    fwd.clear()
    bwd.clear()

    loads[0].wait()
    loads[1].wait()

    def own_state(h):
        own_f[h] = mm_tn(k[:, cols(h)], v[:, cols(h)]).reshape(PARTS, PIECE, DH)

    own_state(other_base)

    pl.semaphore_wait(barrier, jnp.where(has_third, count + 1, count))

    fwd.offer(0)

    def first_states(j, c):
        h = other_base + j
        own_state(h)
        fwd.offer(j)
        return c
    lax.fori_loop(1, half, first_states, 0)

    def own_states(j, c):
        h = own_base + j
        own_state(h)
        return c
    lax.fori_loop(0, half, own_states, 0)

    loads[2].wait()
    low = lax.broadcasted_iota(jnp.int32, (tile, tile), 0) >= lax.broadcasted_iota(
        jnp.int32, (tile, tile), 1)
    up = lax.broadcasted_iota(jnp.int32, (tile, tile), 0) <= lax.broadcasted_iota(
        jnp.int32, (tile, tile), 1)

    def keep(mask, x):
        return jnp.where(mask, x, 0.0).astype(BF16)

    def split(ref, h):
        return ref[0:tile, cols(h)], ref[tile:rows, cols(h)]

    def local_fwd(h, c):
        q0, q1 = split(q, h)
        k0, k1 = split(k, h)
        v0, v1 = split(v, h)
        att[0:tile, cols(h)] = mm(keep(low, mm_nt(q0, k0)), v0)
        att[tile:rows, cols(h)] = mm(mm_nt(q1, k0).astype(BF16), v0) + mm(
            keep(low, mm_nt(q1, k1)), v1)
        q_turned[h] = jnp.transpose(q[:, cols(h)])
        stored[h, 0] = keep(up, mm_nt(k0, q0))
        stored[h, 1] = mm_nt(k0, q1).astype(BF16)
        stored[h, 2] = keep(up, mm_nt(k1, q1))
        return c

    done = fwd.chain(local_fwd, heads, 2 * fwd.at, jnp.where(fwd.at == n_outer - 1, 1, 0), 0)
    lax.fori_loop(done, heads, local_fwd, 0)

    loads[3].wait()
    loads[4].wait()

    def attend(h, sums):
        square, dot = sums
        a = att[:, cols(h)] + mm(q[:, cols(h)], state_bf[h])
        att[:, cols(h)] = a
        scaled = og[:, cols(h)].astype(F32) * gain_ref[0:1, cols(h)]
        return square + a * a, dot + scaled * a

    def attend_own(j, sums):
        return attend(own_base + j, sums)

    def attend_other(j, sums):
        fwd.arrive(j, 0)
        return attend(other_base + j, sums)

    zero = jnp.zeros((rows, DH), F32)
    sums = lax.fori_loop(0, half, attend_own, (zero, zero))
    square, dot = lax.fori_loop(0, half, attend_other, sums)
    square_row = jnp.sum(jnp.transpose(square), axis=0, keepdims=True)
    dot_row = jnp.sum(jnp.transpose(dot), axis=0, keepdims=True)
    stats[...] = jnp.where(
        lax.broadcasted_iota(jnp.int32, (8, rows), 0) == 0, square_row, dot_row)

    def head_copy(r):
        return remote(stats, stats_in.at[r - 1], head_send.at[r - 1], head_recv.at[r - 1],
                      {"head": (hd + r) % n_head})

    for r in range(1, n_head):
        head_copy(r).start()
    total = stats[...]
    for r in range(1, n_head):
        head_copy(r).wait_recv()
        total = total + stats_in[r - 1]
    inverse = lax.rsqrt(total[0:1, :] / columns + norm_eps)
    dot_mean = total[1:2, :] * inverse / columns
    inverse_wide[...] = jnp.transpose(jnp.broadcast_to(inverse, (DH, rows)))
    mean_wide[...] = jnp.transpose(jnp.broadcast_to(dot_mean, (DH, rows)))

    def normalise(h):
        wide = og[:, cols(h)].astype(F32)
        gain = gain_ref[0:1, cols(h)]
        inv = inverse_wide[...]
        normed = att[:, cols(h)] * inv
        outv[:, cols(h)] = (normed * gain).astype(BF16)
        part = (wide * normed).reshape(rows // 8, 8, DH)
        gain_parts[0, :, cols(h)] = jnp.sum(part, axis=0)
        g = (inv * (wide * gain - normed * mean_wide[...])).astype(BF16)
        grad[:, cols(h)] = g
        own_b[h] = mm(q_turned[h], g).reshape(PARTS, PIECE, DH)

    def norm_other(j, c):
        normalise(other_base + j)
        bwd.offer(j)
        return c
    lax.fori_loop(0, half, norm_other, 0)

    def norm_own(j, c):
        normalise(own_base + j)
        return c
    lax.fori_loop(0, half, norm_own, 0)

    out_store = pltpu.make_async_copy(outv, out_hbm, store_sem.at[0])
    out_store.start()

    def gain_copy(level):
        return remote(gain_parts.at[level], gain_in.at[level], gain_send.at[level],
                      gain_recv.at[level], {"seq": level_peer(level)})

    gain_copy(0).start()

    def value_part(h):
        g0, g1 = split(grad, h)
        gv_part[0:tile, cols(h)] = mm(stored[h, 0], g0) + mm(stored[h, 1], g1)
        gv_part[tile:rows, cols(h)] = mm(stored[h, 2], g1)

    def query_part(h):
        k0, k1 = split(k, h)
        v0, v1 = split(v, h)
        g0, g1 = split(grad, h)
        state = state_bf[h]
        gqv[0:tile, cols(h)] = (
            mm_nt(g0, state) + mm(keep(low, mm_nt(g0, v0)), k0)).astype(BF16)
        gqv[tile:rows, cols(h)] = (
            mm_nt(g1, state) + mm(mm_nt(g1, v0).astype(BF16), k0)
            + mm(keep(low, mm_nt(g1, v1)), k1)).astype(BF16)

    def key_part(h):
        q0, q1 = split(q, h)
        v0, v1 = split(v, h)
        g0, g1 = split(grad, h)
        gk_part[0:tile, cols(h)] = mm(keep(up, mm_nt(v0, g0)), q0) + mm(
            mm_nt(v0, g1).astype(BF16), q1)
        gk_part[tile:rows, cols(h)] = mm(keep(up, mm_nt(v1, g1)), q1)

    units = 3 * heads

    def local_bwd(u, c):
        @pl.when(u < heads)
        def _():
            value_part(u)

        @pl.when(jnp.logical_and(u >= heads, u < 2 * heads))
        def _():
            key_part(u - heads)

        @pl.when(u >= 2 * heads)
        def _():
            query_part(u - 2 * heads)
        return c

    def gain_level(level):
        gain_copy(level).wait_recv()
        gain_parts[level + 1] = gain_parts[level] + gain_in[level]
        if level < n_levels - 1:
            gain_copy(level + 1).start()

    done = bwd.chain(local_bwd, units, 2 * bwd.at, jnp.where(bwd.at == n_outer - 1, 2, 0), heads)
    gain_level(0)
    lax.fori_loop(done, units, local_bwd, 0)
    for level in range(1, min(2, n_levels)):
        gain_level(level)

    gq_store = pltpu.make_async_copy(gqv, gq_hbm, store_sem.at[1])
    gq_store.start()

    def finish(h):
        suffix = state_bf[heads + h]
        gkv[:, cols(h)] = (gk_part[:, cols(h)] + mm_nt(v[:, cols(h)], suffix)).astype(BF16)
        gvv[:, cols(h)] = (gv_part[:, cols(h)] + mm(k[:, cols(h)], suffix)).astype(BF16)

    def finish_own(j, c):
        finish(own_base + j)
        return c
    lax.fori_loop(0, half, finish_own, 0)

    span = half * DH
    own_cols = pl.ds(pl.multiple_of(own_base * DH, span), span)
    other_cols = pl.ds(pl.multiple_of(other_base * DH, span), span)
    stores = [
        pltpu.make_async_copy(src.at[:, c], dst.at[:, c], store_sem.at[2 + n])
        for n, (src, dst, c) in enumerate((
            (gkv, gk_hbm, own_cols), (gvv, gv_hbm, own_cols),
            (gkv, gk_hbm, other_cols), (gvv, gv_hbm, other_cols)))
    ]
    stores[0].start()
    stores[1].start()

    def finish_other(j, c):
        bwd.arrive(j, heads)
        finish(other_base + j)
        return c
    lax.fori_loop(0, half, finish_other, 0)
    stores[2].start()
    stores[3].start()

    for level in range(2, n_levels):
        gain_level(level)
    gg_ref[...] = jnp.sum(gain_parts[n_levels], axis=0, keepdims=True)

    fwd.drain()
    bwd.drain()
    for r in range(1, n_head):
        head_copy(r).wait_send()
    for level in range(n_levels):
        gain_copy(level).wait_send()
    out_store.wait()
    gq_store.wait()
    for copy in stores:
        copy.wait()


def write_out(*refs):
    sems = refs[10]
    copies = [pltpu.make_async_copy(refs[n], refs[5 + n], sems.at[n]) for n in range(5)]
    for copy in copies:
        copy.start()
    for copy in copies:
        copy.wait()


def body(n_seq, n_head, query_rows, key_rows, value_rows, norm_gain, out_grad):
    rows, width = query_rows.shape
    heads = width // DH
    half = heads // 2
    tile = rows // 2
    levels = n_seq.bit_length() - 1
    wide = jax.ShapeDtypeStruct((rows, width), BF16)
    vmem = pl.BlockSpec(memory_space=pltpu.VMEM)
    hbm = pl.BlockSpec(memory_space=pl.ANY)
    full = pltpu.VMEM((rows, width), BF16)
    full32 = pltpu.VMEM((rows, width), F32)
    half_states = pltpu.VMEM((half, PARTS, PIECE, DH), F32)
    outs = pl.pallas_call(
        functools.partial(kernel, n_seq, n_head),
        out_shape=[wide] * 4 + [jax.ShapeDtypeStruct((1, width), F32)],
        in_specs=[hbm] * 5,
        out_specs=[hbm] * 4 + [vmem],
        scratch_shapes=[full, full, full, full, pltpu.VMEM((1, width), F32), full32, full,
                        pltpu.VMEM((heads, 3, tile, tile), BF16),
                        full, full, full, full, full32, full32]
        + [pltpu.VMEM((heads, PARTS, PIECE, DH), F32)] * 2
        + [half_states] * 10
        + [
            pltpu.VMEM((heads, DH, rows), BF16),
            pltpu.VMEM((rows, DH), F32),
            pltpu.VMEM((rows, DH), F32),
            pltpu.VMEM((2 * heads, DH, DH), BF16),
            pltpu.VMEM((8, rows), F32),
            pltpu.VMEM((n_head - 1, 8, rows), F32),
            pltpu.VMEM((levels + 1, 8, width), F32),
            pltpu.VMEM((levels, 8, width), F32),
            pltpu.SemaphoreType.DMA((5,)),
            pltpu.SemaphoreType.DMA((6,)),
            pltpu.SemaphoreType.DMA((3, half, PARTS)),
            pltpu.SemaphoreType.DMA((3, half, PARTS)),
            pltpu.SemaphoreType.DMA((3, half, PARTS)),
            pltpu.SemaphoreType.DMA((3, half, PARTS)),
            pltpu.SemaphoreType.DMA((n_head - 1,)),
            pltpu.SemaphoreType.DMA((n_head - 1,)),
            pltpu.SemaphoreType.DMA((levels,)),
            pltpu.SemaphoreType.DMA((levels,)),
        ],
        compiler_params=pltpu.CompilerParams(
            collective_id=0, has_side_effects=True, vmem_limit_bytes=48 * 1024 * 1024),
    )(query_rows, key_rows, value_rows, norm_gain.reshape(1, width), out_grad)
    outs = pl.pallas_call(
        write_out,
        out_shape=[jax.ShapeDtypeStruct(o.shape, o.dtype) for o in outs],
        in_specs=[hbm] * 5,
        out_specs=[hbm] * 5,
        scratch_shapes=[pltpu.SemaphoreType.DMA((5,))],
        compiler_params=pltpu.CompilerParams(vmem_limit_bytes=1024 * 1024),
    )(*outs)
    return (*outs[:4], outs[4].reshape(width))


def solution(mesh):
    in_specs = (P("seq", "head"), P("seq", "head"), P("seq", "head"), P("head"), P("seq", "head"))
    out_specs = (P("seq", "head"), P("seq", "head"), P("seq", "head"), P("seq", "head"), P("head"))
    return jax.shard_map(
        functools.partial(body, mesh.shape["seq"], mesh.shape["head"]),
        mesh=mesh, in_specs=in_specs, out_specs=out_specs, check_vma=False)
```

```python
import functools

import jax
import jax.numpy as jnp
from jax import lax
from jax.experimental import pallas as pl
from jax.experimental.pallas import tpu as pltpu
from jax.sharding import PartitionSpec as P

DH = 128
PARTS = 2
PIECE = DH // PARTS
norm_eps = 1e-06
MESH = pl.DeviceIdType.MESH
F32 = jnp.float32
BF16 = jnp.bfloat16


def mm(a, b):
    return lax.dot_general(a, b, (((1,), (0,)), ((), ())), preferred_element_type=F32)


def mm_nt(a, b):
    return lax.dot_general(a, b, (((1,), (1,)), ((), ())), preferred_element_type=F32)


def mm_tn(a, b):
    return lax.dot_general(a, b, (((0,), (0,)), ((), ())), preferred_element_type=F32)


def kernel(
    n_seq, n_head, q_hbm, k_hbm, v_hbm, gain_hbm, og_hbm,
    out_hbm, gq_hbm, gk_hbm, gv_hbm, gg_ref,
    q, k, v, og, gain_ref, att, grad, stored, outv, gqv, gkv, gvv, gk_part, gv_part,
    own_f, own_b, xr_f, xr_b, zr_f, zr_b, zs_f, zs_b, ys_f, ys_b, yr_f, yr_b,
    q_turned, inverse_wide, mean_wide, state_bf, stats, stats_in, gain_parts, gain_in,
    load_sem, store_sem, send_f, recv_f, send_b, recv_b,
    head_send, head_recv, gain_send, gain_recv,
):
    me = lax.axis_index("seq")
    hd = lax.axis_index("head")
    rows, width = q.shape
    heads = width // DH
    half = heads // 2
    tile = rows // 2
    columns = width * n_head
    n_outer = n_seq // 2
    outer = me // 2
    inner = me % 2
    partner = me + 1 - 2 * inner
    n_levels = gain_in.shape[0]

    loads = [
        pltpu.make_async_copy(src, dst, load_sem.at[j])
        for j, (src, dst) in enumerate((
            (k_hbm, k), (v_hbm, v), (q_hbm, q), (og_hbm, og), (gain_hbm, gain_ref)))
    ]
    for copy in loads:
        copy.start()

    def level_peer(level):
        step = 2 ** level
        bit = (me // step) % 2
        return me + step - 2 * step * bit

    barrier = pltpu.get_barrier_semaphore()
    count = 0
    for r in range(1, n_head):
        pl.semaphore_signal(
            barrier, inc=1, device_id={"head": (hd + r) % n_head}, device_id_type=MESH)
        count += 1
    for level in range(n_levels):
        pl.semaphore_signal(
            barrier, inc=1, device_id={"seq": level_peer(level)}, device_id_type=MESH)
        count += 1

    odd = outer % 2
    third = outer - 1 + 2 * odd
    has_third = jnp.logical_and(third >= 0, third < n_outer)

    @pl.when(has_third)
    def _():
        pl.semaphore_signal(
            barrier, inc=1, device_id={"seq": 2 * third + inner}, device_id_type=MESH)

    def cols(h):
        return pl.ds(pl.multiple_of(h * DH, DH), DH)

    own_base = inner * half
    other_base = (1 - inner) * half

    def remote(src, dst, send, recv, peer):
        return pltpu.make_async_remote_copy(
            src_ref=src, dst_ref=dst, send_sem=send, recv_sem=recv,
            device_id=peer, device_id_type=MESH)

    class Scan:
        def __init__(self, reverse, own, xr, zr, zs, ys, yr, send, recv):
            self.own, self.xr, self.zr, self.zs, self.ys, self.yr = own, xr, zr, zs, ys, yr
            self.send, self.recv = send, recv
            self.at = n_outer - 1 - outer if reverse else outer
            self.side = 1 - inner if reverse else inner
            self.next = me - 2 if reverse else me + 2

        def x(self, j, p):
            return remote(self.own.at[other_base + j, p], self.xr.at[j, p],
                          self.send.at[0, j, p], self.recv.at[0, j, p], {"seq": partner})

        def z(self, j, p):
            return remote(self.zs.at[j, p], self.zr.at[j, p],
                          self.send.at[1, j, p], self.recv.at[1, j, p], {"seq": self.next})

        def y(self, j, p):
            return remote(self.ys.at[j, p], self.yr.at[j, p],
                          self.send.at[2, j, p], self.recv.at[2, j, p], {"seq": partner})

        def clear(self):
            @pl.when(self.at == 0)
            def _():
                self.zr[...] = jnp.zeros_like(self.zr)

        def offer(self, j):
            for p in range(PARTS):
                self.x(j, p).start()

        def step(self, j, p):
            self.x(j, p).wait_recv()

            @pl.when(self.at > 0)
            def _():
                self.z(j, p).wait_recv()

            before = self.zr[j, p]
            mine = self.own[own_base + j, p]
            theirs = self.xr[j, p]

            @pl.when(self.at < n_outer - 1)
            def _():
                self.zs[j, p] = before + (mine + theirs)
                self.z(j, p).start()

            self.ys[j, p] = jnp.where(self.side == 0, before + mine, before)
            self.y(j, p).start()
            return jnp.where(self.side == 0, before, before + theirs)

        def chain(self, local, units, base, between, offset):
            def body(j, c):
                begin = jnp.where(j == 0, 0, jnp.minimum(units, base + (j - 1) * between))
                lax.fori_loop(begin, jnp.minimum(units, base + j * between), local, 0)
                for p in range(PARTS):
                    state_bf[offset + own_base + j, p * PIECE:(p + 1) * PIECE] = self.step(
                        j, p).astype(BF16)
                return c
            lax.fori_loop(0, half, body, 0)
            return jnp.minimum(units, base + (half - 1) * between)

        def arrive(self, j, offset):
            for p in range(PARTS):
                self.y(j, p).wait_recv()
                state_bf[offset + other_base + j, p * PIECE:(p + 1) * PIECE] = self.yr[
                    j, p].astype(BF16)

        def drain(self):
            def body(j, c):
                for p in range(PARTS):
                    self.x(j, p).wait_send()
                    self.y(j, p).wait_send()

                @pl.when(self.at < n_outer - 1)
                def _():
                    for p in range(PARTS):
                        self.z(j, p).wait_send()
                return c
            lax.fori_loop(0, half, body, 0)

    fwd = Scan(False, own_f, xr_f, zr_f, zs_f, ys_f, yr_f, send_f, recv_f)
    bwd = Scan(True, own_b, xr_b, zr_b, zs_b, ys_b, yr_b, send_b, recv_b)
    fwd.clear()
    bwd.clear()

    loads[0].wait()
    loads[1].wait()

    def own_state(h):
        own_f[h] = mm_tn(k[:, cols(h)], v[:, cols(h)]).reshape(PARTS, PIECE, DH)

    own_state(other_base)

    pl.semaphore_wait(barrier, jnp.where(has_third, count + 1, count))

    fwd.offer(0)

    def first_states(j, c):
        h = other_base + j
        own_state(h)
        fwd.offer(j)
        return c
    lax.fori_loop(1, half, first_states, 0)

    def own_states(j, c):
        h = own_base + j
        own_state(h)
        return c
    lax.fori_loop(0, half, own_states, 0)

    loads[2].wait()
    low = lax.broadcasted_iota(jnp.int32, (tile, tile), 0) >= lax.broadcasted_iota(
        jnp.int32, (tile, tile), 1)
    up = lax.broadcasted_iota(jnp.int32, (tile, tile), 0) <= lax.broadcasted_iota(
        jnp.int32, (tile, tile), 1)

    def keep(mask, x):
        return jnp.where(mask, x, 0.0).astype(BF16)

    def split(ref, h):
        return ref[0:tile, cols(h)], ref[tile:rows, cols(h)]

    def local_fwd(h, c):
        q0, q1 = split(q, h)
        k0, k1 = split(k, h)
        v0, v1 = split(v, h)
        att[0:tile, cols(h)] = mm(keep(low, mm_nt(q0, k0)), v0)
        att[tile:rows, cols(h)] = mm(mm_nt(q1, k0).astype(BF16), v0) + mm(
            keep(low, mm_nt(q1, k1)), v1)
        q_turned[h] = jnp.transpose(q[:, cols(h)])
        stored[h, 0] = keep(up, mm_nt(k0, q0))
        stored[h, 1] = mm_nt(k0, q1).astype(BF16)
        stored[h, 2] = keep(up, mm_nt(k1, q1))
        return c

    done = fwd.chain(local_fwd, heads, 1 + 2 * fwd.at, 1, 0)
    lax.fori_loop(done, heads, local_fwd, 0)

    loads[3].wait()
    loads[4].wait()

    def attend(h, sums):
        square, dot = sums
        a = att[:, cols(h)] + mm(q[:, cols(h)], state_bf[h])
        att[:, cols(h)] = a
        scaled = og[:, cols(h)].astype(F32) * gain_ref[0:1, cols(h)]
        return square + a * a, dot + scaled * a

    def attend_own(j, sums):
        return attend(own_base + j, sums)

    def attend_other(j, sums):
        fwd.arrive(j, 0)
        return attend(other_base + j, sums)

    zero = jnp.zeros((rows, DH), F32)
    sums = lax.fori_loop(0, half, attend_own, (zero, zero))
    square, dot = lax.fori_loop(0, half, attend_other, sums)
    square_row = jnp.sum(jnp.transpose(square), axis=0, keepdims=True)
    dot_row = jnp.sum(jnp.transpose(dot), axis=0, keepdims=True)
    stats[...] = jnp.where(
        lax.broadcasted_iota(jnp.int32, (8, rows), 0) == 0, square_row, dot_row)

    def head_copy(r):
        return remote(stats, stats_in.at[r - 1], head_send.at[r - 1], head_recv.at[r - 1],
                      {"head": (hd + r) % n_head})

    for r in range(1, n_head):
        head_copy(r).start()
    total = stats[...]
    for r in range(1, n_head):
        head_copy(r).wait_recv()
        total = total + stats_in[r - 1]
    inverse = lax.rsqrt(total[0:1, :] / columns + norm_eps)
    dot_mean = total[1:2, :] * inverse / columns
    inverse_wide[...] = jnp.transpose(jnp.broadcast_to(inverse, (DH, rows)))
    mean_wide[...] = jnp.transpose(jnp.broadcast_to(dot_mean, (DH, rows)))

    def normalise(h):
        wide = og[:, cols(h)].astype(F32)
        gain = gain_ref[0:1, cols(h)]
        inv = inverse_wide[...]
        normed = att[:, cols(h)] * inv
        outv[:, cols(h)] = (normed * gain).astype(BF16)
        part = (wide * normed).reshape(rows // 8, 8, DH)
        gain_parts[0, :, cols(h)] = jnp.sum(part, axis=0)
        g = (inv * (wide * gain - normed * mean_wide[...])).astype(BF16)
        grad[:, cols(h)] = g
        own_b[h] = mm(q_turned[h], g).reshape(PARTS, PIECE, DH)

    def norm_other(j, c):
        normalise(other_base + j)
        bwd.offer(j)
        return c
    lax.fori_loop(0, half, norm_other, 0)

    def norm_own(j, c):
        normalise(own_base + j)
        return c
    lax.fori_loop(0, half, norm_own, 0)

    out_store = pltpu.make_async_copy(outv, out_hbm, store_sem.at[0])
    out_store.start()

    def gain_copy(level):
        return remote(gain_parts.at[level], gain_in.at[level], gain_send.at[level],
                      gain_recv.at[level], {"seq": level_peer(level)})

    gain_copy(0).start()

    def value_part(h):
        g0, g1 = split(grad, h)
        gv_part[0:tile, cols(h)] = mm(stored[h, 0], g0) + mm(stored[h, 1], g1)
        gv_part[tile:rows, cols(h)] = mm(stored[h, 2], g1)

    def query_part(h):
        k0, k1 = split(k, h)
        v0, v1 = split(v, h)
        g0, g1 = split(grad, h)
        state = state_bf[h]
        gqv[0:tile, cols(h)] = (
            mm_nt(g0, state) + mm(keep(low, mm_nt(g0, v0)), k0)).astype(BF16)
        gqv[tile:rows, cols(h)] = (
            mm_nt(g1, state) + mm(mm_nt(g1, v0).astype(BF16), k0)
            + mm(keep(low, mm_nt(g1, v1)), k1)).astype(BF16)

    def key_part(h):
        q0, q1 = split(q, h)
        v0, v1 = split(v, h)
        g0, g1 = split(grad, h)
        gk_part[0:tile, cols(h)] = mm(keep(up, mm_nt(v0, g0)), q0) + mm(
            mm_nt(v0, g1).astype(BF16), q1)
        gk_part[tile:rows, cols(h)] = mm(keep(up, mm_nt(v1, g1)), q1)

    units = 3 * heads

    def local_bwd(u, c):
        @pl.when(u < heads)
        def _():
            value_part(u)

        @pl.when(jnp.logical_and(u >= heads, u < 2 * heads))
        def _():
            key_part(u - heads)

        @pl.when(u >= 2 * heads)
        def _():
            query_part(u - 2 * heads)
        return c

    def gain_level(level):
        gain_copy(level).wait_recv()
        gain_parts[level + 1] = gain_parts[level] + gain_in[level]
        if level < n_levels - 1:
            gain_copy(level + 1).start()

    done = bwd.chain(local_bwd, units, 3 * bwd.at, jnp.where(bwd.at == n_outer - 1, 3, 0), heads)
    gain_level(0)
    lax.fori_loop(done, units, local_bwd, 0)
    for level in range(1, min(2, n_levels)):
        gain_level(level)

    gq_store = pltpu.make_async_copy(gqv, gq_hbm, store_sem.at[1])
    gq_store.start()

    def finish(h):
        suffix = state_bf[heads + h]
        gkv[:, cols(h)] = (gk_part[:, cols(h)] + mm_nt(v[:, cols(h)], suffix)).astype(BF16)
        gvv[:, cols(h)] = (gv_part[:, cols(h)] + mm(k[:, cols(h)], suffix)).astype(BF16)

    def finish_own(j, c):
        finish(own_base + j)
        return c
    lax.fori_loop(0, half, finish_own, 0)

    span = half * DH
    own_cols = pl.ds(pl.multiple_of(own_base * DH, span), span)
    other_cols = pl.ds(pl.multiple_of(other_base * DH, span), span)
    stores = [
        pltpu.make_async_copy(src.at[:, c], dst.at[:, c], store_sem.at[2 + n])
        for n, (src, dst, c) in enumerate((
            (gkv, gk_hbm, own_cols), (gvv, gv_hbm, own_cols),
            (gkv, gk_hbm, other_cols), (gvv, gv_hbm, other_cols)))
    ]
    stores[0].start()
    stores[1].start()

    def finish_other(j, c):
        bwd.arrive(j, heads)
        finish(other_base + j)
        return c
    lax.fori_loop(0, half, finish_other, 0)
    stores[2].start()
    stores[3].start()

    for level in range(2, n_levels):
        gain_level(level)
    gg_ref[...] = jnp.sum(gain_parts[n_levels], axis=0, keepdims=True)

    fwd.drain()
    bwd.drain()
    for r in range(1, n_head):
        head_copy(r).wait_send()
    for level in range(n_levels):
        gain_copy(level).wait_send()
    out_store.wait()
    gq_store.wait()
    for copy in stores:
        copy.wait()


def write_out(*refs):
    sems = refs[10]
    copies = [pltpu.make_async_copy(refs[n], refs[5 + n], sems.at[n]) for n in range(5)]
    for copy in copies:
        copy.start()
    for copy in copies:
        copy.wait()


def body(n_seq, n_head, query_rows, key_rows, value_rows, norm_gain, out_grad):
    rows, width = query_rows.shape
    heads = width // DH
    half = heads // 2
    tile = rows // 2
    levels = n_seq.bit_length() - 1
    wide = jax.ShapeDtypeStruct((rows, width), BF16)
    vmem = pl.BlockSpec(memory_space=pltpu.VMEM)
    hbm = pl.BlockSpec(memory_space=pl.ANY)
    full = pltpu.VMEM((rows, width), BF16)
    full32 = pltpu.VMEM((rows, width), F32)
    half_states = pltpu.VMEM((half, PARTS, PIECE, DH), F32)
    outs = pl.pallas_call(
        functools.partial(kernel, n_seq, n_head),
        out_shape=[wide] * 4 + [jax.ShapeDtypeStruct((1, width), F32)],
        in_specs=[hbm] * 5,
        out_specs=[hbm] * 4 + [vmem],
        scratch_shapes=[full, full, full, full, pltpu.VMEM((1, width), F32), full32, full,
                        pltpu.VMEM((heads, 3, tile, tile), BF16),
                        full, full, full, full, full32, full32]
        + [pltpu.VMEM((heads, PARTS, PIECE, DH), F32)] * 2
        + [half_states] * 10
        + [
            pltpu.VMEM((heads, DH, rows), BF16),
            pltpu.VMEM((rows, DH), F32),
            pltpu.VMEM((rows, DH), F32),
            pltpu.VMEM((2 * heads, DH, DH), BF16),
            pltpu.VMEM((8, rows), F32),
            pltpu.VMEM((n_head - 1, 8, rows), F32),
            pltpu.VMEM((levels + 1, 8, width), F32),
            pltpu.VMEM((levels, 8, width), F32),
            pltpu.SemaphoreType.DMA((5,)),
            pltpu.SemaphoreType.DMA((6,)),
            pltpu.SemaphoreType.DMA((3, half, PARTS)),
            pltpu.SemaphoreType.DMA((3, half, PARTS)),
            pltpu.SemaphoreType.DMA((3, half, PARTS)),
            pltpu.SemaphoreType.DMA((3, half, PARTS)),
            pltpu.SemaphoreType.DMA((n_head - 1,)),
            pltpu.SemaphoreType.DMA((n_head - 1,)),
            pltpu.SemaphoreType.DMA((levels,)),
            pltpu.SemaphoreType.DMA((levels,)),
        ],
        compiler_params=pltpu.CompilerParams(
            collective_id=0, has_side_effects=True, vmem_limit_bytes=48 * 1024 * 1024),
    )(query_rows, key_rows, value_rows, norm_gain.reshape(1, width), out_grad)
    outs = pl.pallas_call(
        write_out,
        out_shape=[jax.ShapeDtypeStruct(o.shape, o.dtype) for o in outs],
        in_specs=[hbm] * 5,
        out_specs=[hbm] * 5,
        scratch_shapes=[pltpu.SemaphoreType.DMA((5,))],
        compiler_params=pltpu.CompilerParams(vmem_limit_bytes=1024 * 1024),
    )(*outs)
    return (*outs[:4], outs[4].reshape(width))


def solution(mesh):
    in_specs = (P("seq", "head"), P("seq", "head"), P("seq", "head"), P("head"), P("seq", "head"))
    out_specs = (P("seq", "head"), P("seq", "head"), P("seq", "head"), P("seq", "head"), P("head"))
    return jax.shard_map(
        functools.partial(body, mesh.shape["seq"], mesh.shape["head"]),
        mesh=mesh, in_specs=in_specs, out_specs=out_specs, check_vma=False)
```
